512 devices in a mesh: cells: 128 (over z, x, core), slab: 4 (over y).
Axes of the slice: x: 4, y: 4, z: 16, core: 2. Of those that a mesh axis runs over, the one named last changes fastest.
Arguments:
- held_modes: bfloat16 [131072, 1024], P(('cells', 'slab')), may hold values from -5 to 5
- snapshots: bfloat16 [131072, 512], P(('cells', 'slab')), may hold values from -203 to 203
Outputs:
- basis_panel: float32 [131072, 512], P(('cells', 'slab'))
- factor_r: float32 [512, 512], replicated
The draws below stay inside these ranges and needn't reach their ends.
All inputs are finite; a program needn't handle non-finite values.
Results may differ from the reference program's by a relative error of at most 0.0006.
Values sent between devices are 32-bit elements; how exact they have to be, the bound alone decides.
No kernel may reach another device: no remote copies, remote signals or barrier semaphores. Data moves between devices by JAX's collectives and lax.ppermute only.
A program may use at most 64 MiB of HBM per device.

```python
import math
import jax
import jax.numpy as jnp
from jax import lax

K = 1024
P_SIZE = 512
ROWS_DEV = 256
ROWS = 131072


def shared_modes(key):
    return jax.random.truncated_normal(key, -5.0, 5.0, (ROWS, K), jnp.float32)


def draw_held_modes(key, part):
    return shared_modes(key).astype(jnp.bfloat16)


def draw_snapshots(key, part):
    modes_full = shared_modes(key)
    key = jax.random.fold_in(key, 7)
    keys = jax.random.split(key, 5)
    leading = jax.random.uniform(keys[0], (1, P_SIZE), jnp.float32, 1.0, 3.0)
    second = jax.random.uniform(keys[1], (1, P_SIZE), jnp.float32, -1.5, 1.5)
    position = jnp.arange(ROWS, dtype=jnp.float32) / ROWS
    row_scale = jnp.exp(jax.random.uniform(keys[2], (ROWS, 1), jnp.float32, math.log(0.5), math.log(5.0)))
    row_scale = row_scale * (1.0 + 2.0 * position)[:, None]
    column_scale = jnp.exp(jax.random.uniform(keys[3], (1, P_SIZE), jnp.float32, math.log(0.3), math.log(3.0)))
    noise = jax.random.truncated_normal(keys[4], -4.0, 4.0, (ROWS, P_SIZE), jnp.float32)
    values = modes_full[:, :P_SIZE] * leading + modes_full[:, P_SIZE:2 * P_SIZE] * second + row_scale * column_scale * noise
    return values.astype(jnp.bfloat16)


def setup_inputs(seed: int = 0) -> dict:
    seeds = jax.random.split(jax.random.key(seed), 3)
    return {
        "held_modes": draw_held_modes(jax.random.fold_in(seeds[2], 71), 0),
        "snapshots": draw_snapshots(jax.random.fold_in(seeds[2], 71), 0),
    }


def reference(held_modes, snapshots):
    blocks = ROWS // ROWS_DEV
    mode_blocks = held_modes.reshape(blocks, ROWS_DEV, K)
    snap_blocks = snapshots.reshape(blocks, ROWS_DEV, P_SIZE)

    def project(running, pair):
        mode_block, snap_block = pair
        term = lax.dot_general(mode_block.astype(jnp.float32), snap_block.astype(jnp.float32), (((0,), (0,)), ((), ())), preferred_element_type=jnp.float32)
        return (running + term, None)
    summed, _ = lax.scan(project, jnp.zeros((K, P_SIZE), jnp.float32), (mode_blocks, snap_blocks))
    coefficients = summed / ROWS

    def residual_of(mode_block, snap_block):
        return snap_block.astype(jnp.float32) - jnp.dot(mode_block.astype(jnp.float32), coefficients, precision=lax.Precision.HIGHEST)

    def accumulate(running, pair):
        residual_block = residual_of(pair[0], pair[1])
        term = lax.dot_general(residual_block, residual_block, (((0,), (0,)), ((), ())), precision=lax.Precision.HIGHEST)
        return (running + term, None)
    gram_sum, _ = lax.scan(accumulate, jnp.zeros((P_SIZE, P_SIZE), jnp.float32), (mode_blocks, snap_blocks))
    gram = gram_sum / ROWS
    lower_factor = jnp.linalg.cholesky(gram)

    def solve_block(pair):
        residual_block = residual_of(pair[0], pair[1])
        return lax.linalg.triangular_solve(lower_factor, residual_block, left_side=False, lower=True, transpose_a=True)
    basis_panel = lax.map(solve_block, (mode_blocks, snap_blocks)).reshape(ROWS, P_SIZE)
    return (basis_panel, lower_factor.T)
```

```python
import jax
import jax.numpy as jnp
from jax import lax
from jax.sharding import Mesh, PartitionSpec as P

AXES = ("zh", "zl", "x", "core", "y")
SHAPE = (4, 4, 4, 2, 4)
PLANE = ("x", "y")
BLOCK = 128


def exchange(parts, axes):
    return lax.all_to_all(parts, axes, 0, 0, tiled=False)


def scatter_sum(array, axes, count):
    rows = array.shape[0] // count
    return exchange(array.reshape(count, rows, array.shape[1]), axes).sum(0)


def gather(array, axes, count):
    return exchange(jnp.broadcast_to(array[None], (count,) + array.shape), axes)


def swap_cores(array):
    return lax.ppermute(array, "core", [(0, 1), (1, 0)])


def sum_everywhere(array):
    half = array.shape[0] // 2
    core = lax.axis_index("core")
    mine = lax.dynamic_slice_in_dim(array, core * half, half, 0)
    other = lax.dynamic_slice_in_dim(array, (1 - core) * half, half, 0)
    part = scatter_sum(mine + swap_cores(other), PLANE, 16)
    part = gather(part, "zl", 4).sum(0)
    part = gather(part, "zh", 4).sum(0)
    mine = gather(part, PLANE, 16).reshape(half, array.shape[1])
    other = swap_cores(mine)
    first = jnp.where(core == 0, mine, other)
    second = jnp.where(core == 0, other, mine)
    return jnp.concatenate([first, second], 0)


def local(held_modes, snapshots):
    total_rows = held_modes.shape[0] * lax.axis_size(AXES)
    columns = snapshots.shape[1]
    local_terms = lax.dot_general(
        held_modes, snapshots, (((0,), (0,)), ((), ())), preferred_element_type=jnp.float32
    )
    coefficients = sum_everywhere(local_terms) / total_rows
    residual_panel = snapshots.astype(jnp.float32) - jnp.dot(
        held_modes.astype(jnp.float32), coefficients, precision=lax.Precision.HIGHEST
    )
    packed = []
    for start in range(0, columns, BLOCK):
        packed.append(
            lax.dot_general(
                residual_panel[:, : start + BLOCK],
                residual_panel[:, start : start + BLOCK],
                (((0,), (0,)), ((), ())),
                precision=lax.Precision.HIGHEST,
            )
        )
    packed = sum_everywhere(jnp.concatenate(packed, 0)) / total_rows
    upper, row = [], 0
    for start in range(0, columns, BLOCK):
        piece = packed[row : row + start + BLOCK]
        row += start + BLOCK
        upper.append(jnp.pad(piece, ((0, columns - start - BLOCK), (0, 0))))
    upper = jnp.concatenate(upper, 1)
    lower = jnp.where(
        lax.broadcasted_iota(jnp.int32, upper.shape, 0) >= lax.broadcasted_iota(jnp.int32, upper.shape, 1),
        upper.T,
        upper,
    )
    lower_factor = lax.linalg.cholesky(lower, symmetrize_input=False)
    basis_panel = lax.linalg.triangular_solve(
        lower_factor, residual_panel, left_side=False, lower=True, transpose_a=True
    )
    return (basis_panel, lower_factor.T)


def solution(mesh):
    fine = Mesh(mesh.devices.reshape(SHAPE), AXES)
    spec = P(AXES, None)
    return jax.shard_map(local, mesh=fine, in_specs=(spec, spec), out_specs=(spec, P()), check_vma=False)
```

```python
import functools

import jax
import jax.numpy as jnp
from jax import lax
from jax.experimental import pallas as pl
from jax.experimental.pallas import tpu as pltpu
from jax.sharding import Mesh, PartitionSpec as P

AXES = ("zh", "zl", "x", "core", "y")
SHAPE = (4, 4, 4, 2, 4)
PLANE = ("x", "y")
BLOCK = 128
GROUP = 16


def exchange(parts, axes):
    return lax.all_to_all(parts, axes, 0, 0, tiled=False)


def scatter_sum(array, axes, count):
    rows = array.shape[0] // count
    return exchange(array.reshape(count, rows, array.shape[1]), axes).sum(0)


def gather(array, axes, count):
    return exchange(jnp.broadcast_to(array[None], (count,) + array.shape), axes)


def swap_cores(array):
    return lax.ppermute(array, "core", [(0, 1), (1, 0)])


def sum_everywhere(array):
    half = array.shape[0] // 2
    core = lax.axis_index("core")
    mine = lax.dynamic_slice_in_dim(array, core * half, half, 0)
    other = lax.dynamic_slice_in_dim(array, (1 - core) * half, half, 0)
    part = scatter_sum(mine + swap_cores(other), PLANE, 16)
    part = gather(part, "zl", 4).sum(0)
    part = gather(part, "zh", 4).sum(0)
    mine = gather(part, PLANE, 16).reshape(half, array.shape[1])
    other = swap_cores(mine)
    first = jnp.where(core == 0, mine, other)
    second = jnp.where(core == 0, other, mine)
    return jnp.concatenate([first, second], 0)


def product(first, second, first_dim, second_dim):
    return lax.dot_general(
        first,
        second,
        (((first_dim,), (second_dim,)), ((), ())),
        precision=lax.Precision.HIGHEST,
        preferred_element_type=jnp.float32,
    )


def factor_block(block):
    count, wide = BLOCK // GROUP, 2 * BLOCK
    sub = lax.broadcasted_iota(jnp.int32, (GROUP, wide), 0)
    diagonal = lax.broadcasted_iota(jnp.int32, (GROUP, BLOCK), 1) - sub[:, :BLOCK]
    groups = []
    for g in range(count):
        identity = jnp.where(diagonal == GROUP * g, 1.0, 0.0)
        groups.append(jnp.concatenate([block[GROUP * g : GROUP * (g + 1)], identity], 1))
    done = []
    for b in range(count):
        pivots = groups[b]
        columns = [
            jnp.broadcast_to(pivots[:, GROUP * b + k : GROUP * b + k + 1], (GROUP, BLOCK)) for k in range(GROUP)
        ]
        upper = jnp.zeros((GROUP, wide), jnp.float32)
        rows = []
        for k in range(GROUP):
            inverse = lax.rsqrt(columns[k][k : k + 1])
            lower = columns[k] * jnp.broadcast_to(inverse, (GROUP, BLOCK))
            row = jnp.broadcast_to(pivots[k : k + 1] * jnp.concatenate([inverse, inverse], 1), (GROUP, wide))
            rows.append(row)
            upper = jnp.where(sub == k, row, upper)
            if k < GROUP - 1:
                pivots = pivots - jnp.concatenate([lower, lower], 1) * row
                for j in range(k + 1, GROUP):
                    columns[j] = columns[j] - lower * jnp.broadcast_to(columns[j][k : k + 1] * inverse, (GROUP, BLOCK))
        done.append(upper)
        if b < count - 1:
            turned = upper[:, :BLOCK].T
            for g in range(b + 1, count):
                later = groups[g]
                for k in range(GROUP):
                    later = later - jnp.broadcast_to(turned[GROUP * g : GROUP * (g + 1), k : k + 1], (GROUP, wide)) * rows[k]
                groups[g] = later
    done = jnp.concatenate(done, 0)
    order = lax.broadcasted_iota(jnp.int32, (BLOCK, BLOCK), 1) - lax.broadcasted_iota(jnp.int32, (BLOCK, BLOCK), 0)
    return jnp.where(order >= 0, done[:, :BLOCK], 0.0), jnp.where(order <= 0, done[:, BLOCK:], 0.0)


def factor_kernel(packed_ref, residual_ref, basis_ref, upper_ref, gram, *, scale):
    blocks = gram.shape[0] // BLOCK
    upper_ref[...] = jnp.zeros_like(upper_ref)
    basis_ref[...] = residual_ref[...]
    start = 0
    for j in range(blocks):
        rows = BLOCK * (j + 1)
        gram[:rows, rows - BLOCK : rows] = packed_ref[start : start + rows] * scale
        start += rows
    for j in range(blocks):
        low, high = BLOCK * j, BLOCK * (j + 1)
        upper, inverse = factor_block(gram[low:high, low:high])
        upper_ref[low:high, low:high] = upper
        if j < blocks - 1:
            right = product(inverse, gram[low:high, high:], 1, 0)
            upper_ref[low:high, high:] = right
            for i in range(j + 1, blocks):
                first, last = BLOCK * i, BLOCK * (i + 1)
                gram[first:last, first:] -= product(right[:, first - high : last - high], right[:, first - high :], 0, 0)
        piece = product(basis_ref[:, low:high], inverse, 1, 1)
        basis_ref[:, low:high] = piece
        if j < blocks - 1:
            basis_ref[:, high:] -= product(piece, right, 1, 0)


def factor_and_solve(packed, residual_panel, scale):
    columns = residual_panel.shape[1]
    vmem = pl.BlockSpec(memory_space=pltpu.VMEM)
    return pl.pallas_call(
        functools.partial(factor_kernel, scale=scale),
        out_shape=(
            jax.ShapeDtypeStruct(residual_panel.shape, jnp.float32),
            jax.ShapeDtypeStruct((columns, columns), jnp.float32),
        ),
        in_specs=[vmem, vmem],
        out_specs=[vmem, vmem],
        scratch_shapes=[pltpu.VMEM((columns, columns), jnp.float32)],
        compiler_params=pltpu.CompilerParams(vmem_limit_bytes=24 << 20),
    )(packed, residual_panel)


def local(held_modes, snapshots):
    total_rows = held_modes.shape[0] * lax.axis_size(AXES)
    columns = snapshots.shape[1]
    local_terms = lax.dot_general(
        held_modes, snapshots, (((0,), (0,)), ((), ())), preferred_element_type=jnp.float32
    )
    coefficients = sum_everywhere(local_terms) / total_rows
    residual_panel = snapshots.astype(jnp.float32) - jnp.dot(
        held_modes.astype(jnp.float32), coefficients, precision=lax.Precision.HIGHEST
    )
    packed = []
    for start in range(0, columns, BLOCK):
        packed.append(
            lax.dot_general(
                residual_panel[:, : start + BLOCK],
                residual_panel[:, start : start + BLOCK],
                (((0,), (0,)), ((), ())),
                precision=lax.Precision.HIGHEST,
            )
        )
    packed = sum_everywhere(jnp.concatenate(packed, 0))
    return factor_and_solve(packed, residual_panel, 1.0 / total_rows)


def solution(mesh):
    fine = Mesh(mesh.devices.reshape(SHAPE), AXES)
    spec = P(AXES, None)
    return jax.shard_map(local, mesh=fine, in_specs=(spec, spec), out_specs=(spec, P()), check_vma=False)
```

```python
import functools

import jax
import jax.numpy as jnp
from jax import lax
from jax.experimental import pallas as pl
from jax.experimental.pallas import tpu as pltpu
from jax.sharding import Mesh, PartitionSpec as P

AXES = ("zh", "zl", "x", "core", "y")
SHAPE = (4, 4, 4, 2, 4)
PLANE = ("x", "y")
BLOCK = 128
GROUP = 16
TILE = 8


def exchange(parts, axes):
    return lax.all_to_all(parts, axes, 0, 0, tiled=False)


def scatter_sum(array, axes, count):
    rows = array.shape[0] // count
    return exchange(array.reshape(count, rows, array.shape[1]), axes).sum(0)


def gather(array, axes, count):
    return exchange(jnp.broadcast_to(array[None], (count,) + array.shape), axes)


def swap_cores(array):
    return lax.ppermute(array, "core", [(0, 1), (1, 0)])


def sum_modes(mine, other):
    part = scatter_sum(mine + swap_cores(other), PLANE, 16)
    part = gather(part, "zl", 4).sum(0)
    part = gather(part, "zh", 4).sum(0)
    return gather(part, PLANE, 16).reshape(mine.shape)


def sum_gram(mine, other):
    part = scatter_sum(mine + swap_cores(other), PLANE, 16)
    part = gather(part, ("zh", "zl"), 16).sum(0)
    half = gather(part, PLANE, 16).reshape(mine.shape)
    return lax.all_gather(half, "core", axis=0, tiled=True)


def residual_kernel(core_ref, modes_ref, snapshots_ref, own_ref, far_ref, residual_ref, mine_ref, other_ref, *, scale):
    core = core_ref[0]
    half = modes_ref.shape[1] // 2
    total = jnp.zeros(snapshots_ref.shape, jnp.float32)
    for place, coefficients_ref in ((core, own_ref), (1 - core, far_ref)):
        modes = modes_ref[:, pl.ds(pl.multiple_of(place * half, half), half)]
        rest = coefficients_ref[...]
        for _ in range(3):
            term = rest.astype(jnp.bfloat16)
            rest = rest - term.astype(jnp.float32)
            total += lax.dot_general(modes, term, (((1,), (0,)), ((), ())), preferred_element_type=jnp.float32)
    residual = snapshots_ref[...].astype(jnp.float32) - total * scale
    residual_ref[...] = residual
    blocks = residual.shape[1] // BLOCK
    rows = mine_ref.shape[0]
    start = 0
    for j in range(blocks):
        piece = product(residual[:, : BLOCK * (j + 1)], residual[:, BLOCK * j : BLOCK * (j + 1)], 0, 0)
        for i in range(j + 1):
            side, place = divmod(start, rows)
            value = piece[BLOCK * i : BLOCK * (i + 1)]

            @pl.when(core == side)
            def _(place=place, value=value):
                mine_ref[place : place + BLOCK] = value

            @pl.when(core != side)
            def _(place=place, value=value):
                other_ref[place : place + BLOCK] = value

            start += BLOCK


def residual_and_gram(core, modes, snapshots, own, far, scale):
    columns = snapshots.shape[1]
    blocks = columns // BLOCK
    half = jax.ShapeDtypeStruct((blocks * (blocks + 1) // 4 * BLOCK, BLOCK), jnp.float32)
    vmem = pl.BlockSpec(memory_space=pltpu.VMEM)
    return pl.pallas_call(
        functools.partial(residual_kernel, scale=scale),
        out_shape=(jax.ShapeDtypeStruct(snapshots.shape, jnp.float32), half, half),
        in_specs=[pl.BlockSpec(memory_space=pltpu.SMEM), vmem, vmem, vmem, vmem],
        out_specs=[vmem, vmem, vmem],
        compiler_params=pltpu.CompilerParams(vmem_limit_bytes=24 << 20),
    )(core.reshape(1), modes, snapshots, own, far)


def product(first, second, first_dim, second_dim):
    return lax.dot_general(
        first,
        second,
        (((first_dim,), (second_dim,)), ((), ())),
        precision=lax.Precision.HIGHEST,
        preferred_element_type=jnp.float32,
    )


def spread(array, row):
    return jnp.broadcast_to(array[row : row + 1], (TILE, array.shape[1]))


def factor_block(block):
    tiles, per_group = BLOCK // TILE, GROUP // TILE
    sub = lax.broadcasted_iota(jnp.int32, (TILE, 2 * BLOCK), 0)
    diagonal = lax.broadcasted_iota(jnp.int32, (TILE, BLOCK), 1) - sub[:, :BLOCK]
    work = []
    for t in range(tiles):
        identity = jnp.where(diagonal == TILE * t, 1.0, 0.0)
        work.append(jnp.concatenate([block[TILE * t : TILE * (t + 1)], identity], 1))
    done = []
    for first in range(0, tiles, per_group):
        near = work[first : first + 2 * per_group]
        start = TILE * first
        columns = [
            [jnp.broadcast_to(tile[:, start + k : start + k + 1], (TILE, BLOCK)) for tile in near] for k in range(GROUP)
        ]
        upper = [jnp.zeros((TILE, 2 * BLOCK), jnp.float32)] * per_group
        pivot = spread(columns[0][0], 0)
        for k in range(GROUP):
            tile, row = divmod(k, TILE)
            root = lax.rsqrt(pivot)
            inverse = root * root
            pivot_row = spread(near[tile], row)
            upper[tile] = jnp.where(sub == row, pivot_row * jnp.concatenate([root, root], 1), upper[tile])
            if k < GROUP - 1:
                off = spread(columns[k + 1][tile], row)
                pivot = spread(columns[k + 1][(k + 1) // TILE], (k + 1) % TILE) - (off * off) * inverse
            heads = {j: spread(columns[j][tile], row) for j in range(k + 1, GROUP)}
            for t in range(tile, len(near)):
                if t == tile and row == TILE - 1:
                    continue
                factor = columns[k][t] * inverse
                near[t] = near[t] - jnp.concatenate([factor, factor], 1) * pivot_row
                for j in range(k + 1, GROUP):
                    columns[j][t] = columns[j][t] - factor * heads[j]
        work[first + per_group : first + 2 * per_group] = near[per_group:]
        upper = jnp.concatenate(upper, 0)
        done.append(upper)
        far = first + 2 * per_group
        if far < tiles:
            update = product(upper[:, TILE * far : BLOCK], upper, 0, 0)
            for t in range(far, tiles):
                work[t] = work[t] - update[TILE * (t - far) : TILE * (t - far + 1)]
    done = jnp.concatenate(done, 0)
    order = lax.broadcasted_iota(jnp.int32, (BLOCK, BLOCK), 1) - lax.broadcasted_iota(jnp.int32, (BLOCK, BLOCK), 0)
    return jnp.where(order >= 0, done[:, :BLOCK], 0.0), jnp.where(order <= 0, done[:, BLOCK:], 0.0)


def factor_kernel(packed_ref, residual_ref, basis_ref, upper_ref, gram, *, scale):
    blocks = gram.shape[0] // BLOCK
    upper_ref[...] = jnp.zeros_like(upper_ref)
    basis_ref[...] = residual_ref[...]
    start = 0
    for j in range(blocks):
        rows = BLOCK * (j + 1)
        gram[:rows, rows - BLOCK : rows] = packed_ref[start : start + rows] * scale
        start += rows
    for j in range(blocks):
        low, high = BLOCK * j, BLOCK * (j + 1)
        upper, inverse = factor_block(gram[low:high, low:high])
        upper_ref[low:high, low:high] = upper
        if j < blocks - 1:
            right = product(inverse, gram[low:high, high:], 1, 0)
            upper_ref[low:high, high:] = right
            for i in range(j + 1, blocks):
                first, last = BLOCK * i, BLOCK * (i + 1)
                gram[first:last, first:] -= product(right[:, first - high : last - high], right[:, first - high :], 0, 0)
        piece = product(basis_ref[:, low:high], inverse, 1, 1)
        basis_ref[:, low:high] = piece
        if j < blocks - 1:
            basis_ref[:, high:] -= product(piece, right, 1, 0)


def factor_and_solve(packed, residual_panel, scale):
    columns = residual_panel.shape[1]
    vmem = pl.BlockSpec(memory_space=pltpu.VMEM)
    return pl.pallas_call(
        functools.partial(factor_kernel, scale=scale),
        out_shape=(
            jax.ShapeDtypeStruct(residual_panel.shape, jnp.float32),
            jax.ShapeDtypeStruct((columns, columns), jnp.float32),
        ),
        in_specs=[vmem, vmem],
        out_specs=[vmem, vmem],
        scratch_shapes=[pltpu.VMEM((columns, columns), jnp.float32)],
        compiler_params=pltpu.CompilerParams(vmem_limit_bytes=24 << 20),
    )(packed, residual_panel)


def local(held_modes, snapshots):
    scale = 1.0 / (held_modes.shape[0] * lax.axis_size(AXES))
    core = lax.axis_index("core")
    half = held_modes.shape[1] // 2

    def terms(place):
        modes = lax.dynamic_slice_in_dim(held_modes, place * half, half, 1)
        return lax.dot_general(modes, snapshots, (((0,), (0,)), ((), ())), preferred_element_type=jnp.float32)

    other = terms(1 - core)
    own = sum_modes(terms(core), other)
    far = swap_cores(own)
    residual_panel, mine, other = residual_and_gram(core, held_modes, snapshots, own, far, scale)
    return factor_and_solve(sum_gram(mine, other), residual_panel, scale)


def solution(mesh):
    fine = Mesh(mesh.devices.reshape(SHAPE), AXES)
    spec = P(AXES, None)
    return jax.shard_map(local, mesh=fine, in_specs=(spec, spec), out_specs=(spec, P()), check_vma=False)
```

```python
import functools

import jax
import jax.numpy as jnp
from jax import lax
from jax.experimental import pallas as pl
from jax.experimental.pallas import tpu as pltpu
from jax.sharding import Mesh, PartitionSpec as P

AXES = ("zh", "zl", "x", "core", "y")
SHAPE = (4, 4, 4, 2, 4)
PLANE = ("x", "y")
BLOCK = 128
GROUP = 16
TILE = 8


def exchange(parts, axes):
    return lax.all_to_all(parts, axes, 0, 0, tiled=False)


def scatter_sum(array, axes, count):
    rows = array.shape[0] // count
    return exchange(array.reshape(count, rows, array.shape[1]), axes).sum(0)


def gather(array, axes, count):
    return exchange(jnp.broadcast_to(array[None], (count,) + array.shape), axes)


def swap_cores(array):
    return lax.ppermute(array, "core", [(0, 1), (1, 0)])


def sum_modes(mine, other):
    part = scatter_sum(mine + swap_cores(other), PLANE, 16)
    part = gather(part, "zl", 4).sum(0)
    part = gather(part, "zh", 4).sum(0)
    return gather(part, PLANE, 16).reshape(mine.shape)


def sum_gram(mine, arrived):
    part = scatter_sum(mine + arrived, PLANE, 16)
    part = gather(part, ("zh", "zl"), 16).sum(0)
    half = gather(part, PLANE, 16).reshape(mine.shape)
    return lax.all_gather(half, "core", axis=0, tiled=True)


def mode_products(modes_ref, place, coefficients):
    half = modes_ref.shape[1] // 2
    modes = modes_ref[:, pl.ds(pl.multiple_of(place * half, half), half)]
    total = 0.0
    for term in three_terms(coefficients):
        total += lax.dot_general(modes, term, (((1,), (0,)), ((), ())), preferred_element_type=jnp.float32)
    return total


def own_kernel(core_ref, modes_ref, own_ref, partial_ref):
    partial_ref[...] = mode_products(modes_ref, core_ref[0], own_ref[...])


def gram_half(residual, side, out_ref):
    if side == 0:
        wide = product(residual[:, : 2 * BLOCK], residual[:, BLOCK : 3 * BLOCK], 0, 0)
        out_ref[:BLOCK] = product(residual[:, :BLOCK], residual[:, :BLOCK], 0, 0)
        out_ref[BLOCK : 3 * BLOCK] = wide[:, :BLOCK]
        out_ref[3 * BLOCK :] = wide[:, BLOCK:]
    else:
        third = residual[:, 2 * BLOCK : 3 * BLOCK]
        out_ref[:BLOCK] = product(third, third, 0, 0)
        out_ref[BLOCK:] = product(residual, residual[:, 3 * BLOCK :], 0, 0)


def residual_kernel(core_ref, modes_ref, snapshots_ref, partial_ref, far_ref, residual_ref, other_ref, *, scale):
    core = core_ref[0]
    total = partial_ref[...] + mode_products(modes_ref, 1 - core, far_ref[...])
    residual_ref[...] = snapshots_ref[...].astype(jnp.float32) - total * scale
    for side in range(2):

        @pl.when(core != side)
        def _(side=side):
            gram_half(residual_ref[...], side, other_ref)


def mine_kernel(core_ref, residual_ref, mine_ref):
    for side in range(2):

        @pl.when(core_ref[0] == side)
        def _(side=side):
            gram_half(residual_ref[...], side, mine_ref)


def call_kernel(kernel, core, arrays, out_shapes, flops):
    vmem = pl.BlockSpec(memory_space=pltpu.VMEM)
    shapes = [jax.ShapeDtypeStruct(shape, jnp.float32) for shape in out_shapes]
    return pl.pallas_call(
        kernel,
        out_shape=shapes,
        in_specs=[pl.BlockSpec(memory_space=pltpu.SMEM)] + [vmem] * len(arrays),
        out_specs=[vmem] * len(shapes),
        cost_estimate=pl.CostEstimate(flops=flops, bytes_accessed=1 << 20, transcendentals=0),
        compiler_params=pltpu.CompilerParams(vmem_limit_bytes=24 << 20),
    )(core.reshape(1), *arrays)


def three_terms(array):
    terms = []
    for _ in range(3):
        terms.append(array.astype(jnp.bfloat16))
        array = array - terms[-1].astype(jnp.float32)
    return terms


def product(first, second, first_dim, second_dim):
    high, middle, low = three_terms(first)
    left = jnp.concatenate([high, high, middle, middle, high, low], first_dim)
    high, middle, low = three_terms(second)
    right = jnp.concatenate([high, middle, high, middle, low, high], second_dim)
    return lax.dot_general(
        left, right, (((first_dim,), (second_dim,)), ((), ())), preferred_element_type=jnp.float32
    )


def spread(array, row):
    return jnp.broadcast_to(array[row : row + 1], (TILE, array.shape[1]))


def factor_block(block):
    tiles, per_group = BLOCK // TILE, GROUP // TILE
    sub = lax.broadcasted_iota(jnp.int32, (TILE, 2 * BLOCK), 0)
    diagonal = lax.broadcasted_iota(jnp.int32, (TILE, BLOCK), 1) - sub[:, :BLOCK]
    work = []
    for t in range(tiles):
        identity = jnp.where(diagonal == TILE * t, 1.0, 0.0)
        work.append(jnp.concatenate([block[TILE * t : TILE * (t + 1)], identity], 1))
    done = []
    for first in range(0, tiles, per_group):
        near = work[first : first + 2 * per_group]
        start = TILE * first
        columns = [
            [jnp.broadcast_to(tile[:, start + k : start + k + 1], (TILE, BLOCK)) for tile in near] for k in range(GROUP)
        ]
        upper = [jnp.zeros((TILE, 2 * BLOCK), jnp.float32)] * per_group
        pivot = spread(columns[0][0], 0)
        for k in range(GROUP):
            tile, row = divmod(k, TILE)
            root = lax.rsqrt(pivot)
            inverse = root * root
            pivot_row = spread(near[tile], row)
            upper[tile] = jnp.where(sub == row, pivot_row * jnp.concatenate([root, root], 1), upper[tile])
            if k < GROUP - 1:
                off = spread(columns[k + 1][tile], row)
                pivot = spread(columns[k + 1][(k + 1) // TILE], (k + 1) % TILE) - (off * off) * inverse
            heads = {j: spread(columns[j][tile], row) for j in range(k + 1, GROUP)}
            for t in range(tile, len(near)):
                if t == tile and row == TILE - 1:
                    continue
                factor = columns[k][t] * inverse
                near[t] = near[t] - jnp.concatenate([factor, factor], 1) * pivot_row
                for j in range(k + 1, GROUP):
                    columns[j][t] = columns[j][t] - factor * heads[j]
        work[first + per_group : first + 2 * per_group] = near[per_group:]
        upper = jnp.concatenate(upper, 0)
        done.append(upper)
        far = first + 2 * per_group
        if far < tiles:
            update = product(upper[:, :BLOCK], upper, 0, 0)
            for t in range(far, tiles):
                work[t] = work[t] - update[TILE * t : TILE * (t + 1)]
    done = jnp.concatenate(done, 0)
    order = lax.broadcasted_iota(jnp.int32, (BLOCK, BLOCK), 1) - lax.broadcasted_iota(jnp.int32, (BLOCK, BLOCK), 0)
    return jnp.where(order >= 0, done[:, :BLOCK], 0.0), jnp.where(order <= 0, done[:, BLOCK:], 0.0)


def factor_kernel(packed_ref, residual_ref, basis_ref, upper_ref, gram, *, scale):
    blocks = gram.shape[0] // BLOCK
    upper_ref[...] = jnp.zeros_like(upper_ref)
    basis_ref[...] = residual_ref[...]
    start = 0
    for j in range(blocks):
        rows = BLOCK * (j + 1)
        gram[:rows, rows - BLOCK : rows] = packed_ref[start : start + rows] * scale
        start += rows
    for j in range(blocks):
        low, high = BLOCK * j, BLOCK * (j + 1)
        upper, inverse = factor_block(gram[low:high, low:high])
        upper_ref[low:high, low:high] = upper
        if j < blocks - 1:
            right = product(inverse, gram[low:high, high:], 1, 0)
            upper_ref[low:high, high:] = right
            for i in range(j + 1, blocks):
                first, last = BLOCK * i, BLOCK * (i + 1)
                gram[first:last, first:] -= product(right[:, first - high : last - high], right[:, first - high :], 0, 0)
        piece = product(basis_ref[:, low:high], inverse, 1, 1)
        basis_ref[:, low:high] = piece
        if j < blocks - 1:
            basis_ref[:, high:] -= product(piece, right, 1, 0)


def factor_and_solve(packed, residual_panel, scale):
    columns = residual_panel.shape[1]
    vmem = pl.BlockSpec(memory_space=pltpu.VMEM)
    return pl.pallas_call(
        functools.partial(factor_kernel, scale=scale),
        out_shape=(
            jax.ShapeDtypeStruct(residual_panel.shape, jnp.float32),
            jax.ShapeDtypeStruct((columns, columns), jnp.float32),
        ),
        in_specs=[vmem, vmem],
        out_specs=[vmem, vmem],
        scratch_shapes=[pltpu.VMEM((columns, columns), jnp.float32)],
        compiler_params=pltpu.CompilerParams(vmem_limit_bytes=24 << 20),
    )(packed, residual_panel)


def local(held_modes, snapshots):
    scale = 1.0 / (held_modes.shape[0] * lax.axis_size(AXES))
    core = lax.axis_index("core")
    half = held_modes.shape[1] // 2

    def terms(place):
        modes = lax.dynamic_slice_in_dim(held_modes, place * half, half, 1)
        return lax.dot_general(modes, snapshots, (((0,), (0,)), ((), ())), preferred_element_type=jnp.float32)

    other = terms(1 - core)
    own = sum_modes(terms(core), other)
    far = swap_cores(own)
    rows, columns = snapshots.shape
    half_gram = (columns * (columns // BLOCK + 1) // 4, BLOCK)
    flops = 6 * rows * half * columns
    (partial,) = call_kernel(own_kernel, core, (held_modes, own), ((rows, columns),), flops)
    residual_panel, other = call_kernel(
        functools.partial(residual_kernel, scale=scale),
        core,
        (held_modes, snapshots, partial, far),
        ((rows, columns), half_gram),
        2 * flops,
    )
    arrived = swap_cores(other)
    (mine,) = call_kernel(mine_kernel, core, (residual_panel,), (half_gram,), flops)
    return factor_and_solve(sum_gram(mine, arrived), residual_panel, scale)


def solution(mesh):
    fine = Mesh(mesh.devices.reshape(SHAPE), AXES)
    spec = P(AXES, None)
    return jax.shard_map(local, mesh=fine, in_specs=(spec, spec), out_specs=(spec, P()), check_vma=False)
```

```python
import functools

import jax
import jax.numpy as jnp
from jax import lax
from jax.experimental import pallas as pl
from jax.experimental.pallas import tpu as pltpu
from jax.sharding import Mesh, PartitionSpec as P

AXES = ("zh", "zl", "x", "core", "y")
SHAPE = (4, 4, 4, 2, 4)
PLANE = ("x", "y")
BLOCK = 128
GROUP = 16
TILE = 8


def exchange(parts, axes):
    return lax.all_to_all(parts, axes, 0, 0, tiled=False)


def scatter_sum(array, axes, count):
    rows = array.shape[0] // count
    return exchange(array.reshape(count, rows, array.shape[1]), axes).sum(0)


def gather(array, axes, count):
    return exchange(jnp.broadcast_to(array[None], (count,) + array.shape), axes)


def swap_cores(array):
    return lax.ppermute(array, "core", [(0, 1), (1, 0)])


def sum_modes(mine, arrived):
    part = scatter_sum(mine + arrived, PLANE, 16)
    part = gather(part, "zl", 4).sum(0)
    part = gather(part, "zh", 4).sum(0)
    return gather(part, PLANE, 16).reshape(mine.shape)


def sum_gram(mine, arrived):
    part = scatter_sum(mine + arrived, PLANE, 16)
    part = gather(part, ("zh", "zl"), 16).sum(0)
    half = gather(part, PLANE, 16).reshape(mine.shape)
    return lax.all_gather(half, "core", axis=0, tiled=True)


def mode_products(modes_ref, place, coefficients):
    half = modes_ref.shape[1] // 2
    modes = modes_ref[:, pl.ds(pl.multiple_of(place * half, half), half)]
    total = 0.0
    for term in three_terms(coefficients):
        total += lax.dot_general(modes, term, (((1,), (0,)), ((), ())), preferred_element_type=jnp.float32)
    return total


def terms_kernel(core_ref, modes_ref, snapshots_ref, terms_ref):
    half = modes_ref.shape[1] // 2
    modes = modes_ref[:, pl.ds(pl.multiple_of(core_ref[0] * half, half), half)]
    terms_ref[...] = lax.dot_general(
        modes, snapshots_ref[...], (((0,), (0,)), ((), ())), preferred_element_type=jnp.float32
    )


def own_kernel(core_ref, modes_ref, own_ref, partial_ref):
    partial_ref[...] = mode_products(modes_ref, core_ref[0], own_ref[...])


def gram_half(residual, side, out_ref):
    if side == 0:
        wide = product(residual[:, : 2 * BLOCK], residual[:, BLOCK : 3 * BLOCK], 0, 0)
        out_ref[:BLOCK] = product(residual[:, :BLOCK], residual[:, :BLOCK], 0, 0)
        out_ref[BLOCK : 3 * BLOCK] = wide[:, :BLOCK]
        out_ref[3 * BLOCK :] = wide[:, BLOCK:]
    else:
        third = residual[:, 2 * BLOCK : 3 * BLOCK]
        out_ref[:BLOCK] = product(third, third, 0, 0)
        out_ref[BLOCK:] = product(residual, residual[:, 3 * BLOCK :], 0, 0)


def residual_kernel(core_ref, modes_ref, snapshots_ref, partial_ref, far_ref, residual_ref, other_ref, *, scale):
    core = core_ref[0]
    total = partial_ref[...] + mode_products(modes_ref, 1 - core, far_ref[...])
    residual_ref[...] = snapshots_ref[...].astype(jnp.float32) - total * scale
    for side in range(2):

        @pl.when(core != side)
        def _(side=side):
            gram_half(residual_ref[...], side, other_ref)


def mine_kernel(core_ref, residual_ref, mine_ref):
    for side in range(2):

        @pl.when(core_ref[0] == side)
        def _(side=side):
            gram_half(residual_ref[...], side, mine_ref)


def call_kernel(kernel, core, arrays, out_shapes, flops):
    vmem = pl.BlockSpec(memory_space=pltpu.VMEM)
    shapes = [jax.ShapeDtypeStruct(shape, jnp.float32) for shape in out_shapes]
    return pl.pallas_call(
        kernel,
        out_shape=shapes,
        in_specs=[pl.BlockSpec(memory_space=pltpu.SMEM)] + [vmem] * len(arrays),
        out_specs=[vmem] * len(shapes),
        cost_estimate=pl.CostEstimate(flops=flops, bytes_accessed=1 << 20, transcendentals=0),
        compiler_params=pltpu.CompilerParams(vmem_limit_bytes=24 << 20),
    )(core.reshape(1), *arrays)


def three_terms(array):
    terms = []
    for _ in range(3):
        terms.append(array.astype(jnp.bfloat16))
        array = array - terms[-1].astype(jnp.float32)
    return terms


def product(first, second, first_dim, second_dim):
    high, middle, low = three_terms(first)
    left = jnp.concatenate([high, high, middle, middle, high, low], first_dim)
    high, middle, low = three_terms(second)
    right = jnp.concatenate([high, middle, high, middle, low, high], second_dim)
    return lax.dot_general(
        left, right, (((first_dim,), (second_dim,)), ((), ())), preferred_element_type=jnp.float32
    )


def spread(array, row):
    return jnp.broadcast_to(array[row : row + 1], (TILE, array.shape[1]))


def factor_block(block):
    tiles, per_group = BLOCK // TILE, GROUP // TILE
    sub = lax.broadcasted_iota(jnp.int32, (TILE, 2 * BLOCK), 0)
    diagonal = lax.broadcasted_iota(jnp.int32, (TILE, BLOCK), 1) - sub[:, :BLOCK]
    work = []
    for t in range(tiles):
        identity = jnp.where(diagonal == TILE * t, 1.0, 0.0)
        work.append(jnp.concatenate([block[TILE * t : TILE * (t + 1)], identity], 1))
    done = []
    for first in range(0, tiles, per_group):
        near = work[first : first + 2 * per_group]
        start = TILE * first
        columns = [
            [jnp.broadcast_to(tile[:, start + k : start + k + 1], (TILE, BLOCK)) for tile in near] for k in range(GROUP)
        ]
        upper = [jnp.zeros((TILE, 2 * BLOCK), jnp.float32)] * per_group
        pivot = spread(columns[0][0], 0)
        for k in range(GROUP):
            tile, row = divmod(k, TILE)
            root = lax.rsqrt(pivot)
            inverse = root * root
            pivot_row = spread(near[tile], row)
            upper[tile] = jnp.where(sub == row, pivot_row * jnp.concatenate([root, root], 1), upper[tile])
            if k < GROUP - 1:
                off = spread(columns[k + 1][tile], row)
                pivot = spread(columns[k + 1][(k + 1) // TILE], (k + 1) % TILE) - (off * off) * inverse
            heads = {j: spread(columns[j][tile], row) for j in range(k + 1, GROUP)}
            for t in range(tile, len(near)):
                if t == tile and row == TILE - 1:
                    continue
                factor = columns[k][t] * inverse
                near[t] = near[t] - jnp.concatenate([factor, factor], 1) * pivot_row
                for j in range(k + 1, GROUP):
                    columns[j][t] = columns[j][t] - factor * heads[j]
        work[first + per_group : first + 2 * per_group] = near[per_group:]
        upper = jnp.concatenate(upper, 0)
        done.append(upper)
        far = first + 2 * per_group
        if far < tiles:
            update = product(upper[:, :BLOCK], upper, 0, 0)
            for t in range(far, tiles):
                work[t] = work[t] - update[TILE * t : TILE * (t + 1)]
    done = jnp.concatenate(done, 0)
    order = lax.broadcasted_iota(jnp.int32, (BLOCK, BLOCK), 1) - lax.broadcasted_iota(jnp.int32, (BLOCK, BLOCK), 0)
    return jnp.where(order >= 0, done[:, :BLOCK], 0.0), jnp.where(order <= 0, done[:, BLOCK:], 0.0)


def factor_kernel(packed_ref, residual_ref, basis_ref, upper_ref, gram, *, scale):
    blocks = gram.shape[0] // BLOCK
    upper_ref[...] = jnp.zeros_like(upper_ref)
    basis_ref[...] = residual_ref[...]
    start = 0
    for j in range(blocks):
        rows = BLOCK * (j + 1)
        gram[:rows, rows - BLOCK : rows] = packed_ref[start : start + rows] * scale
        start += rows
    for j in range(blocks):
        low, high = BLOCK * j, BLOCK * (j + 1)
        upper, inverse = factor_block(gram[low:high, low:high])
        upper_ref[low:high, low:high] = upper
        if j < blocks - 1:
            right = product(inverse, gram[low:high, high:], 1, 0)
            upper_ref[low:high, high:] = right
            for i in range(j + 1, blocks):
                first, last = BLOCK * i, BLOCK * (i + 1)
                gram[first:last, first:] -= product(right[:, first - high : last - high], right[:, first - high :], 0, 0)
        piece = product(basis_ref[:, low:high], inverse, 1, 1)
        basis_ref[:, low:high] = piece
        if j < blocks - 1:
            basis_ref[:, high:] -= product(piece, right, 1, 0)


def factor_and_solve(packed, residual_panel, scale):
    columns = residual_panel.shape[1]
    vmem = pl.BlockSpec(memory_space=pltpu.VMEM)
    return pl.pallas_call(
        functools.partial(factor_kernel, scale=scale),
        out_shape=(
            jax.ShapeDtypeStruct(residual_panel.shape, jnp.float32),
            jax.ShapeDtypeStruct((columns, columns), jnp.float32),
        ),
        in_specs=[vmem, vmem],
        out_specs=[vmem, vmem],
        scratch_shapes=[pltpu.VMEM((columns, columns), jnp.float32)],
        compiler_params=pltpu.CompilerParams(vmem_limit_bytes=24 << 20),
    )(packed, residual_panel)


def local(held_modes, snapshots):
    scale = 1.0 / (held_modes.shape[0] * lax.axis_size(AXES))
    core = lax.axis_index("core")
    half = held_modes.shape[1] // 2
    rows, columns = snapshots.shape
    flops = 6 * rows * half * columns
    leaving = lax.dynamic_slice_in_dim(held_modes, (1 - core) * half, half, 1)
    other = lax.dot_general(leaving, snapshots, (((0,), (0,)), ((), ())), preferred_element_type=jnp.float32)
    arrived = swap_cores(other)
    (mine,) = call_kernel(terms_kernel, core, (held_modes, snapshots), ((half, columns),), flops)
    own = sum_modes(mine, arrived)
    far = swap_cores(own)
    half_gram = (columns * (columns // BLOCK + 1) // 4, BLOCK)
    (partial,) = call_kernel(own_kernel, core, (held_modes, own), ((rows, columns),), flops)
    residual_panel, other = call_kernel(
        functools.partial(residual_kernel, scale=scale),
        core,
        (held_modes, snapshots, partial, far),
        ((rows, columns), half_gram),
        2 * flops,
    )
    arrived = swap_cores(other)
    (mine,) = call_kernel(mine_kernel, core, (residual_panel,), (half_gram,), flops)
    return factor_and_solve(sum_gram(mine, arrived), residual_panel, scale)


def solution(mesh):
    fine = Mesh(mesh.devices.reshape(SHAPE), AXES)
    spec = P(AXES, None)
    return jax.shard_map(local, mesh=fine, in_specs=(spec, spec), out_specs=(spec, P()), check_vma=False)
```

```python
import functools

import jax
import jax.numpy as jnp
from jax import lax
from jax.experimental import pallas as pl
from jax.experimental.pallas import tpu as pltpu
from jax.sharding import Mesh, PartitionSpec as P

AXES = ("zh", "zl", "x", "core", "y")
SHAPE = (4, 4, 4, 2, 4)
PLANE = ("x", "y")
BLOCK = 128
GROUP = 16
TILE = 8


def exchange(parts, axes):
    return lax.all_to_all(parts, axes, 0, 0, tiled=False)


def scatter_sum(array, axes, count):
    rows = array.shape[0] // count
    return exchange(array.reshape(count, rows, array.shape[1]), axes).sum(0)


def gather(array, axes, count):
    return exchange(jnp.broadcast_to(array[None], (count,) + array.shape), axes)


def swap_cores(array):
    return lax.ppermute(array, "core", [(0, 1), (1, 0)])


def sum_modes(mine, other):
    part = scatter_sum(mine + swap_cores(other), PLANE, 16)
    part = gather(scatter_sum(part, ("zh", "zl"), 16), ("zh", "zl"), 16).reshape(part.shape)
    return gather(part, PLANE, 16).reshape(mine.shape)


def sum_gram(mine, arrived):
    part = scatter_sum(mine + arrived, PLANE, 16)
    part = gather(part, ("zh", "zl"), 16).sum(0)
    half = gather(part, PLANE, 16).reshape(mine.shape)
    return lax.all_gather(half, "core", axis=0, tiled=True)


def mode_products(modes_ref, place, coefficients):
    half = modes_ref.shape[1] // 2
    modes = modes_ref[:, pl.ds(pl.multiple_of(place * half, half), half)]
    total = 0.0
    for term in three_terms(coefficients):
        total += lax.dot_general(modes, term, (((1,), (0,)), ((), ())), preferred_element_type=jnp.float32)
    return total


def own_kernel(core_ref, modes_ref, own_ref, partial_ref):
    partial_ref[...] = mode_products(modes_ref, core_ref[0], own_ref[...])


def gram_half(residual, side, out_ref):
    if side == 0:
        wide = product(residual[:, : 2 * BLOCK], residual[:, BLOCK : 3 * BLOCK], 0, 0)
        out_ref[:BLOCK] = product(residual[:, :BLOCK], residual[:, :BLOCK], 0, 0)
        out_ref[BLOCK : 3 * BLOCK] = wide[:, :BLOCK]
        out_ref[3 * BLOCK :] = wide[:, BLOCK:]
    else:
        third = residual[:, 2 * BLOCK : 3 * BLOCK]
        out_ref[:BLOCK] = product(third, third, 0, 0)
        out_ref[BLOCK:] = product(residual, residual[:, 3 * BLOCK :], 0, 0)


def residual_kernel(core_ref, modes_ref, snapshots_ref, partial_ref, far_ref, residual_ref, other_ref, *, scale):
    core = core_ref[0]
    total = partial_ref[...] + mode_products(modes_ref, 1 - core, far_ref[...])
    residual_ref[...] = snapshots_ref[...].astype(jnp.float32) - total * scale
    for side in range(2):

        @pl.when(core != side)
        def _(side=side):
            gram_half(residual_ref[...], side, other_ref)


def mine_kernel(core_ref, residual_ref, mine_ref):
    for side in range(2):

        @pl.when(core_ref[0] == side)
        def _(side=side):
            gram_half(residual_ref[...], side, mine_ref)


def call_kernel(kernel, core, arrays, out_shapes, flops):
    vmem = pl.BlockSpec(memory_space=pltpu.VMEM)
    shapes = [jax.ShapeDtypeStruct(shape, jnp.float32) for shape in out_shapes]
    return pl.pallas_call(
        kernel,
        out_shape=shapes,
        in_specs=[pl.BlockSpec(memory_space=pltpu.SMEM)] + [vmem] * len(arrays),
        out_specs=[vmem] * len(shapes),
        cost_estimate=pl.CostEstimate(flops=flops, bytes_accessed=1 << 20, transcendentals=0),
        compiler_params=pltpu.CompilerParams(vmem_limit_bytes=24 << 20),
    )(core.reshape(1), *arrays)


def three_terms(array):
    terms = []
    for _ in range(3):
        terms.append(array.astype(jnp.bfloat16))
        array = array - terms[-1].astype(jnp.float32)
    return terms


def product(first, second, first_dim, second_dim):
    high, middle, low = three_terms(first)
    left = jnp.concatenate([high, high, middle, middle, high, low], first_dim)
    high, middle, low = three_terms(second)
    right = jnp.concatenate([high, middle, high, middle, low, high], second_dim)
    return lax.dot_general(
        left, right, (((first_dim,), (second_dim,)), ((), ())), preferred_element_type=jnp.float32
    )


def spread(array, row):
    return jnp.broadcast_to(array[row : row + 1], (TILE, array.shape[1]))


def factor_block(block):
    tiles, per_group = BLOCK // TILE, GROUP // TILE
    sub = lax.broadcasted_iota(jnp.int32, (TILE, 2 * BLOCK), 0)
    diagonal = lax.broadcasted_iota(jnp.int32, (TILE, BLOCK), 1) - sub[:, :BLOCK]
    work = []
    for t in range(tiles):
        identity = jnp.where(diagonal == TILE * t, 1.0, 0.0)
        work.append(jnp.concatenate([block[TILE * t : TILE * (t + 1)], identity], 1))
    done = []
    for first in range(0, tiles, per_group):
        near = work[first : first + 2 * per_group]
        start = TILE * first
        columns = [
            [jnp.broadcast_to(tile[:, start + k : start + k + 1], (TILE, BLOCK)) for tile in near] for k in range(GROUP)
        ]
        upper = [jnp.zeros((TILE, 2 * BLOCK), jnp.float32)] * per_group
        pivot = spread(columns[0][0], 0)
        for k in range(GROUP):
            tile, row = divmod(k, TILE)
            root = lax.rsqrt(pivot)
            inverse = root * root
            pivot_row = spread(near[tile], row)
            upper[tile] = jnp.where(sub == row, pivot_row * jnp.concatenate([root, root], 1), upper[tile])
            if k < GROUP - 1:
                off = spread(columns[k + 1][tile], row)
                pivot = spread(columns[k + 1][(k + 1) // TILE], (k + 1) % TILE) - (off * off) * inverse
            heads = {j: spread(columns[j][tile], row) for j in range(k + 1, GROUP)}
            for t in range(tile, len(near)):
                if t == tile and row == TILE - 1:
                    continue
                factor = columns[k][t] * inverse
                near[t] = near[t] - jnp.concatenate([factor, factor], 1) * pivot_row
                for j in range(k + 1, GROUP):
                    columns[j][t] = columns[j][t] - factor * heads[j]
        work[first + per_group : first + 2 * per_group] = near[per_group:]
        upper = jnp.concatenate(upper, 0)
        done.append(upper)
        far = first + 2 * per_group
        if far < tiles:
            update = product(upper[:, :BLOCK], upper, 0, 0)
            for t in range(far, tiles):
                work[t] = work[t] - update[TILE * t : TILE * (t + 1)]
    done = jnp.concatenate(done, 0)
    order = lax.broadcasted_iota(jnp.int32, (BLOCK, BLOCK), 1) - lax.broadcasted_iota(jnp.int32, (BLOCK, BLOCK), 0)
    return jnp.where(order >= 0, done[:, :BLOCK], 0.0), jnp.where(order <= 0, done[:, BLOCK:], 0.0)


def factor_kernel(packed_ref, residual_ref, basis_ref, upper_ref, gram, *, scale):
    blocks = gram.shape[0] // BLOCK
    upper_ref[...] = jnp.zeros_like(upper_ref)
    basis_ref[...] = residual_ref[...]
    start = 0
    for j in range(blocks):
        rows = BLOCK * (j + 1)
        gram[:rows, rows - BLOCK : rows] = packed_ref[start : start + rows] * scale
        start += rows
    for j in range(blocks):
        low, high = BLOCK * j, BLOCK * (j + 1)
        upper, inverse = factor_block(gram[low:high, low:high])
        upper_ref[low:high, low:high] = upper
        if j < blocks - 1:
            right = product(inverse, gram[low:high, high:], 1, 0)
            upper_ref[low:high, high:] = right
            for i in range(j + 1, blocks):
                first, last = BLOCK * i, BLOCK * (i + 1)
                gram[first:last, first:] -= product(right[:, first - high : last - high], right[:, first - high :], 0, 0)
        piece = product(basis_ref[:, low:high], inverse, 1, 1)
        basis_ref[:, low:high] = piece
        if j < blocks - 1:
            basis_ref[:, high:] -= product(piece, right, 1, 0)


def factor_and_solve(packed, residual_panel, scale):
    columns = residual_panel.shape[1]
    vmem = pl.BlockSpec(memory_space=pltpu.VMEM)
    return pl.pallas_call(
        functools.partial(factor_kernel, scale=scale),
        out_shape=(
            jax.ShapeDtypeStruct(residual_panel.shape, jnp.float32),
            jax.ShapeDtypeStruct((columns, columns), jnp.float32),
        ),
        in_specs=[vmem, vmem],
        out_specs=[vmem, vmem],
        scratch_shapes=[pltpu.VMEM((columns, columns), jnp.float32)],
        compiler_params=pltpu.CompilerParams(vmem_limit_bytes=24 << 20),
    )(packed, residual_panel)


def local(held_modes, snapshots):
    scale = 1.0 / (held_modes.shape[0] * lax.axis_size(AXES))
    core = lax.axis_index("core")
    half = held_modes.shape[1] // 2

    def terms(place):
        modes = lax.dynamic_slice_in_dim(held_modes, place * half, half, 1)
        return lax.dot_general(modes, snapshots, (((0,), (0,)), ((), ())), preferred_element_type=jnp.float32)

    other = terms(1 - core)
    own = sum_modes(terms(core), other)
    far = swap_cores(own)
    rows, columns = snapshots.shape
    half_gram = (columns * (columns // BLOCK + 1) // 4, BLOCK)
    flops = 6 * rows * half * columns
    (partial,) = call_kernel(own_kernel, core, (held_modes, own), ((rows, columns),), flops)
    residual_panel, other = call_kernel(
        functools.partial(residual_kernel, scale=scale),
        core,
        (held_modes, snapshots, partial, far),
        ((rows, columns), half_gram),
        2 * flops,
    )
    arrived = swap_cores(other)
    (mine,) = call_kernel(mine_kernel, core, (residual_panel,), (half_gram,), flops)
    return factor_and_solve(sum_gram(mine, arrived), residual_panel, scale)


def solution(mesh):
    fine = Mesh(mesh.devices.reshape(SHAPE), AXES)
    spec = P(AXES, None)
    return jax.shard_map(local, mesh=fine, in_specs=(spec, spec), out_specs=(spec, P()), check_vma=False)
```
